32 devices in a mesh: scene: 16 (over z, y, x), veh: 2 (over core).
Axes of the slice: x: 2, y: 2, z: 4, core: 2. Of those that a mesh axis runs over, the one named last changes fastest.
Arguments:
- features: bfloat16 [16, 4, 256, 16, 128], P('scene', 'veh'), may hold values from -64 to 64
- counts: int32 [16], P('scene'), may hold values from 2 to 4, as said below
- ego_ids: int32 [16], P('scene'), may hold values from 0 to 3, as said below
- req_tiles: int32 [16, 4, 2], P('scene', 'veh'), may hold values from 0 to 3, as said below
- req_count: int32 [16, 4], P('scene', 'veh'), may hold values from 1 to 2, as said below
- ego_embed: bfloat16 [256], replicated, may hold values from -8 to 8
- enc_weight: bfloat16 [9, 256, 256], replicated, may hold values from -0.125 to 0.125
- post_weight: bfloat16 [9, 256, 256], replicated, may hold values from -0.125 to 0.125
- cotangent: bfloat16 [16, 256, 16, 128], P('scene', None, 'veh'), may hold values from -6 to 6
Outputs:
- refined: bfloat16 [16, 256, 16, 128], P('scene', None, 'veh')
- feature_grad: float32 [16, 4, 256, 16, 128], P('scene', 'veh')
- enc_grad: float32 [9, 256, 256], replicated
- post_grad: float32 [9, 256, 256], replicated
- embed_grad: float32 [256], replicated
The draws below stay inside these ranges and needn't reach their ends.
Inputs may be any that keep to these rules, and one draw needn't show every extreme that they name: `counts`: some scene has all 4 vehicles. `ego_ids`: the ego is one of the scene's present vehicles; in some scene with all 4 vehicles in which the ego asks 2 tiles of every other vehicle, the ego is the last vehicle. `req_tiles`: the 2 tile ids of one vehicle are distinct. `req_count`: the ego's own entry and those of vehicles at or beyond the count are not used; in some scene with all 4 vehicles the ego asks 2 tiles of every other vehicle.
All inputs are finite; a program needn't handle non-finite values.
Results may differ from the reference program's by a relative error of at most 0.012.
The reference program's roundings to bfloat16 on the way count: a program that leaves them out, or rounds other values in their place, can miss the bound.
Values may be sent and summed in bfloat16 or wider, within the bound.
A program may use at most 192 MiB of HBM per device.

```python
import jax
import jax.numpy as jnp
from jax import lax

C = 256
TILE = 32
ROWS = 16
TCOLS = 4
KMAX = 2
VEH = 4
SCENES = 16


def draw_ints(key):
    count_key, full_key, ego_key, asked_key, score_key = jax.random.split(jax.random.fold_in(key, 5), 5)
    lowest = max(2, VEH - 3)
    scene_ids = jnp.arange(SCENES)
    full_scene = jax.random.randint(full_key, (), 0, SCENES)
    counts = jax.random.randint(count_key, (SCENES,), lowest, VEH + 1)
    counts = jnp.where(scene_ids == full_scene, VEH, counts).astype(jnp.int32)
    ego_ids = jax.random.randint(ego_key, (SCENES,), 0, 1 << 20) % counts
    ego_ids = jnp.where(scene_ids == full_scene, VEH - 1, ego_ids).astype(jnp.int32)
    asked_count = jax.random.randint(asked_key, (SCENES, VEH), 1, KMAX + 1)
    asked_count = jnp.where(scene_ids[:, None] == full_scene, KMAX, asked_count).astype(jnp.int32)
    scores = jax.random.randint(score_key, (SCENES, VEH, TCOLS), 0, 1 << 16) * TCOLS + jnp.arange(TCOLS)
    picked = jnp.argsort(scores, axis=-1)[..., :KMAX].astype(jnp.int32)
    return (counts, ego_ids, picked, asked_count)


def draw_counts(key, part):
    return draw_ints(key)[0]


def draw_ego_ids(key, part):
    return draw_ints(key)[1]


def draw_req_tiles(key, part):
    return draw_ints(key)[2]


def draw_req_count(key, part):
    return draw_ints(key)[3]


def draw_features(key, part):
    base_key = jax.random.fold_in(jax.random.fold_in(key, 11), 0)
    full_shape = (SCENES, VEH, C, ROWS, TILE * TCOLS)
    values = jnp.clip(jax.random.normal(base_key, full_shape, jnp.float32), -6.0, 6.0)
    return values.astype(jnp.bfloat16)


def block_scale(stream_key, dims, cuts, low, top_value):
    def one(position, shards_of):
        heights = jax.random.uniform(jax.random.fold_in(jax.random.fold_in(stream_key, 6), position), (shards_of,), jnp.float32, low / len(cuts), top_value / len(cuts))
        return jnp.repeat(jnp.exp(heights), dims[position] // shards_of).reshape((-1,) + (1,) * (len(dims) - position - 1))

    loudness = one(*cuts[0])
    for cut in cuts[1:]:
        loudness = loudness * one(*cut)
    return loudness


def centred(key, shape, spread, bound, shards=(), dtype=jnp.bfloat16):
    gain = block_scale(key, shape, shards, -0.22, 0.18) if shards else 1.0
    array = jax.random.normal(key, shape, jnp.float32) * spread * gain
    return jnp.minimum(jnp.maximum(array, -bound), bound).astype(dtype)


def setup_inputs(seed: int = 0) -> dict:
    seeds = jax.random.split(jax.random.key(seed), 10)
    features = draw_features(jax.random.fold_in(seeds[9], 71), 0)
    counts = draw_counts(jax.random.fold_in(seeds[9], 71), 0)
    ego_ids = draw_ego_ids(jax.random.fold_in(seeds[9], 71), 0)
    req_tiles = draw_req_tiles(jax.random.fold_in(seeds[9], 71), 0)
    req_count = draw_req_count(jax.random.fold_in(seeds[9], 71), 0)
    ego_embed = centred(seeds[5], (C,), 2.0, 8.0)
    enc_weight = centred(seeds[6], (9, C, C), (9 * C) ** -0.5, 0.125)
    post_weight = centred(seeds[7], (9, C, C), (9 * C) ** -0.5, 0.125)
    cotangent = centred(seeds[8], (SCENES, C, ROWS, TILE * TCOLS), 1.0, 6.0, ((0, 16), (2, 2)))
    return {"features": features, "counts": counts, "ego_ids": ego_ids, "req_tiles": req_tiles, "req_count": req_count, "ego_embed": ego_embed, "enc_weight": enc_weight, "post_weight": post_weight, "cotangent": cotangent}


def pad_rows(source):
    return jnp.pad(source, [(0, 0)] * (source.ndim - 2) + [(2, 2), (0, 0)])


def tap_stack(padded, out_rows):
    breadth = padded.shape[-1]
    widened = jnp.pad(padded, [(0, 0)] * (padded.ndim - 1) + [(2, 2)])
    pieces = []
    for row_tap in range(3):
        for col_tap in range(3):
            pieces.append(widened[..., 2 * row_tap:2 * row_tap + out_rows, 2 * col_tap:2 * col_tap + breadth])
    return jnp.stack(pieces, axis=-4)


def conv_apply(weight, stacked):
    return jnp.einsum("tio,...tirw->...orw", weight.astype(jnp.float32), stacked.astype(jnp.float32), precision=lax.Precision.HIGHEST)


def conv_back(weight, stacked):
    return jnp.einsum("tio,...torw->...irw", weight[::-1].astype(jnp.float32), stacked.astype(jnp.float32), precision=lax.Precision.HIGHEST)


def silu_slope(values):
    sigma = jax.nn.sigmoid(values)
    return sigma * (1.0 + values * (1.0 - sigma))


def join_agents(query, partners, col_mask, ego_embed):
    query_wide = query.astype(jnp.float32)
    parts_wide = partners.astype(jnp.float32)
    channel_count = query.shape[-3]
    key_self = query_wide + ego_embed.astype(jnp.float32)[:, None, None]
    score_self = jnp.sum(query_wide * key_self, axis=-3) / channel_count
    score_part = jnp.sum(query_wide[..., None, :, :, :] * parts_wide, axis=-3) / channel_count
    live_cells = col_mask[..., :, None, :] > 0.5
    row_max = jnp.maximum(score_self, jnp.max(jnp.where(live_cells, score_part, -jnp.inf), axis=-3))
    self_exp = jnp.exp(score_self - row_max)
    part_exp = jnp.where(live_cells, jnp.exp(jnp.minimum(score_part - row_max[..., None, :, :], 0.0)), 0.0)
    denominator = self_exp + jnp.sum(part_exp, axis=-3)
    self_weight = self_exp / denominator
    part_weight = part_exp / denominator[..., None, :, :]
    joined_map = self_weight[..., None, :, :] * query_wide + jnp.sum(part_weight[..., :, None, :, :] * parts_wide, axis=-4)
    return joined_map, self_weight, part_weight


def attend_back(query, partners, ego_embed, self_weight, part_weight, joined_grad):
    query_wide = query.astype(jnp.float32)
    parts_wide = partners.astype(jnp.float32)
    channel_count = query.shape[-3]
    self_dot = jnp.sum(joined_grad * query_wide, axis=-3)
    part_dot = jnp.sum(joined_grad[..., None, :, :, :] * parts_wide, axis=-3)
    mean_dot = self_weight * self_dot + jnp.sum(part_weight * part_dot, axis=-3)
    slope_self = self_weight * (self_dot - mean_dot)
    slope_part = part_weight * (part_dot - mean_dot[..., None, :, :])
    twice_key = 2.0 * query_wide + ego_embed.astype(jnp.float32)[:, None, None]
    ego_term = self_weight[..., None, :, :] * joined_grad + (slope_self[..., None, :, :] * twice_key + jnp.sum(slope_part[..., :, None, :, :] * parts_wide, axis=-4)) / channel_count
    part_grads = part_weight[..., :, None, :, :] * joined_grad[..., None, :, :, :] + slope_part[..., :, None, :, :] * query_wide[..., None, :, :, :] / channel_count
    embed_terms = jnp.sum(slope_self[..., None, :, :] * query_wide, axis=(-2, -1)) / channel_count
    embed_partial = jnp.sum(embed_terms.reshape(-1, channel_count), axis=0)
    return ego_term.astype(jnp.bfloat16), part_grads.astype(jnp.bfloat16), embed_partial


def scene_step(feature_maps, count, ego_id, tiles_asked, asked_count, cot_map, ego_embed, enc_weight, post_weight):
    vehicles, channel_count, height, breadth = feature_maps.shape
    tile_count = breadth // TILE
    veh_ids = jnp.arange(vehicles)
    live_count = jnp.where((veh_ids < count) & (veh_ids != ego_id), asked_count, 0)
    onehot = ((tiles_asked[:, :, None] == jnp.arange(tile_count)[None, None, :]) & (jnp.arange(KMAX)[None, :, None] < live_count[:, None, None])).astype(jnp.float32)
    col_mask = jnp.repeat(jnp.sum(onehot, axis=1), TILE, axis=-1)
    enc_stack = tap_stack(pad_rows(feature_maps), height)
    enc_pre = conv_apply(enc_weight, enc_stack)
    encoded = (feature_maps.astype(jnp.float32) + jax.nn.silu(enc_pre)).astype(jnp.bfloat16)
    ego_map = encoded[ego_id]
    partners = (encoded.astype(jnp.float32) * col_mask[:, None, None, :]).astype(jnp.bfloat16)
    joined_map, self_weight, part_weight = join_agents(ego_map, partners, col_mask, ego_embed)
    joined_bf = joined_map.astype(jnp.bfloat16)
    post_stack = tap_stack(pad_rows(joined_bf), height)
    post_pre = conv_apply(post_weight, post_stack)
    refined = (joined_bf.astype(jnp.float32) + jax.nn.silu(post_pre)).astype(jnp.bfloat16)
    grad_map = cot_map.astype(jnp.float32)
    post_slope = (grad_map * silu_slope(post_pre)).astype(jnp.bfloat16)
    post_partial = jnp.einsum("tirw,orw->tio", post_stack.astype(jnp.float32), post_slope.astype(jnp.float32), precision=lax.Precision.HIGHEST)
    joined_grad = grad_map + conv_back(post_weight, tap_stack(pad_rows(post_slope), height))
    ego_term, part_grads, embed_partial = attend_back(ego_map, partners, ego_embed, self_weight, part_weight, joined_grad)
    is_ego = (veh_ids == ego_id).astype(jnp.float32)[:, None, None, None]
    encoded_grad = part_grads.astype(jnp.float32) + is_ego * ego_term.astype(jnp.float32)[None]
    enc_slope = (encoded_grad * silu_slope(enc_pre)).astype(jnp.bfloat16)
    enc_partial = jnp.einsum("vtirw,vorw->tio", enc_stack.astype(jnp.float32), enc_slope.astype(jnp.float32), precision=lax.Precision.HIGHEST)
    feature_grad = encoded_grad + conv_back(enc_weight, tap_stack(pad_rows(enc_slope), height))
    return refined, feature_grad, enc_partial, post_partial, embed_partial


def reference(features, counts, ego_ids, req_tiles, req_count, ego_embed, enc_weight, post_weight, cotangent):
    def one_scene(inputs):
        feature_maps, count, ego_id, tiles_asked, asked_count, cot_map = inputs
        return scene_step(feature_maps, count, ego_id, tiles_asked, asked_count, cot_map, ego_embed, enc_weight, post_weight)

    refined, feature_grad, enc_parts, post_parts, embed_parts = lax.map(one_scene, (features, counts, ego_ids, req_tiles, req_count, cotangent))
    return refined, feature_grad, jnp.sum(enc_parts, axis=0), jnp.sum(post_parts, axis=0), jnp.sum(embed_parts, axis=0)
```

```python
import jax
import jax.numpy as jnp
from jax import lax
from jax.experimental import pallas as pl
from jax.experimental.pallas import tpu as pltpu
from jax.sharding import PartitionSpec as P

TILE = 32
KMAX = 2
F32 = jnp.float32
BF16 = jnp.bfloat16
LANES = 128
CHUNK = 512
VMEM_LIMIT = 56 * 1024 * 1024


def sigmoid(z):
    return 1.0 / (1.0 + jnp.exp(-z))


def silu_slope(z):
    sig = sigmoid(z)
    return sig * (1.0 + z * (1.0 - sig))


def clear_pads(taps_ref, cells):
    rows = taps_ref.shape[0]
    taps_ref[:, : 2 * LANES] = jnp.zeros((rows, 2 * LANES), BF16)
    taps_ref[:, 2 * LANES + cells :] = jnp.zeros((rows, 2 * LANES), BF16)


def put_row(taps_ref, r, row):
    channels = row.shape[0]
    lane = lax.broadcasted_iota(jnp.int32, row.shape, 1)
    at = slice((r + 2) * LANES, (r + 3) * LANES)
    left = jnp.where(lane >= 2, pltpu.roll(row, 2, 1), 0.0)
    right = jnp.where(lane < LANES - 2, pltpu.roll(row, LANES - 2, 1), 0.0)
    taps_ref[:channels, at] = left.astype(BF16)
    taps_ref[channels : 2 * channels, at] = row.astype(BF16)
    taps_ref[2 * channels :, at] = right.astype(BF16)


def turn_weight(w_ref, wt_ref):
    channels = w_ref.shape[1]
    for t in range(9):
        at = slice(t * channels, (t + 1) * channels)
        wt_ref[:, at] = w_ref[at, :].T


def flip_weight(w_ref, wb_ref):
    channels = w_ref.shape[1]
    for t in range(9):
        wb_ref[:, t * channels : (t + 1) * channels] = w_ref[
            (8 - t) * channels : (9 - t) * channels, :
        ]


def conv_chunk(w_ref, taps_ref, j):
    depth = taps_ref.shape[0]
    total = None
    for a in range(3):
        part = jnp.dot(
            w_ref[:, a * depth : (a + 1) * depth],
            taps_ref[:, a * 2 * LANES + j * CHUNK : a * 2 * LANES + (j + 1) * CHUNK],
            preferred_element_type=F32,
        )
        total = part if total is None else total + part
    return total


def dot_nt(left, right, precision=None):
    return lax.dot_general(
        left, right, (((1,), (1,)), ((), ())), preferred_element_type=F32, precision=precision
    )


def load_map(x_ref, wide_ref, taps_ref, rows):
    channels = taps_ref.shape[0] // 3
    wide_ref[...] = x_ref[0].astype(F32)
    clear_pads(taps_ref, rows * LANES)
    for r in range(rows):
        put_row(taps_ref, r, wide_ref[pl.ds(r, channels, stride=rows), :])


def encode_kernel(x_ref, w_ref, pre_ref, enc_ref, wide_ref, taps_ref, wt_ref):
    channels = w_ref.shape[1]
    cells = pre_ref.shape[-1]
    rows = cells // LANES

    @pl.when(pl.program_id(0) == 0)
    def _():
        turn_weight(w_ref, wt_ref)

    load_map(x_ref, wide_ref, taps_ref, rows)
    for j in range(cells // CHUNK):
        at = slice(j * CHUNK, (j + 1) * CHUNK)
        pre = conv_chunk(wt_ref, taps_ref, j)
        here = taps_ref[channels : 2 * channels, 2 * LANES + j * CHUNK : 2 * LANES + (j + 1) * CHUNK]
        pre_ref[0, :, at] = pre
        enc_ref[0, :, at] = (here.astype(F32) + pre * sigmoid(pre)).astype(BF16)


def encode(x, weight):
    veh, deep, _ = x.shape
    channels = weight.shape[1]
    cells = deep // channels * LANES
    return pl.pallas_call(
        encode_kernel,
        grid=(veh,),
        out_shape=(
            jax.ShapeDtypeStruct((veh, channels, cells), F32),
            jax.ShapeDtypeStruct((veh, channels, cells), BF16),
        ),
        in_specs=[
            pl.BlockSpec((1, deep, LANES), lambda v: (v, 0, 0)),
            pl.BlockSpec((9 * channels, channels), lambda v: (0, 0)),
        ],
        out_specs=(
            pl.BlockSpec((1, channels, cells), lambda v: (v, 0, 0)),
            pl.BlockSpec((1, channels, cells), lambda v: (v, 0, 0)),
        ),
        scratch_shapes=[
            pltpu.VMEM((deep, LANES), F32),
            pltpu.VMEM((3 * channels, cells + 4 * LANES), BF16),
            pltpu.VMEM((channels, 9 * channels), BF16),
        ],
        compiler_params=pltpu.CompilerParams(vmem_limit_bytes=VMEM_LIMIT),
        cost_estimate=pl.CostEstimate(
            flops=2 * veh * 9 * channels * channels * cells,
            bytes_accessed=veh * channels * cells * 8,
            transcendentals=veh * channels * cells,
        ),
        name="encode",
    )(x, weight)


def post_kernel(
    ids_ref, enc_ref, live_ref, embed_ref, cot_ref, w_ref,
    refined_ref, grad_ref, eg_ref,
    wide_ref, cotw_ref, taps_ref, slope_ref, wt_ref, out_ref, weights_ref, jg_ref,
):
    vehicles, channels, cells = enc_ref.shape
    rows = cells // LANES
    half = rows // 2
    local = eg_ref.shape[0]
    ego, me = ids_ref[0], ids_ref[1]
    inv = 1.0 / channels
    turn_weight(w_ref, wt_ref)
    clear_pads(taps_ref, cells)
    clear_pads(slope_ref, cells)
    embed = embed_ref[...]

    def colsum(x):
        return jnp.sum(x, axis=0, keepdims=True)

    for r in range(rows):
        at = slice(r * LANES, (r + 1) * LANES)
        query = enc_ref[ego, :, at].astype(F32)
        score_self = colsum(query * (query + embed)) * inv
        scores, top = [], score_self
        for v in range(vehicles):
            score = colsum(query * enc_ref[v, :, at].astype(F32)) * inv
            live = live_ref[v : v + 1, :] > 0.5
            top = jnp.maximum(top, jnp.where(live, score, -jnp.inf))
            scores.append(score)
        exps = [jnp.exp(score_self - top)]
        for v in range(vehicles):
            live = live_ref[v : v + 1, :] > 0.5
            exps.append(jnp.where(live, jnp.exp(jnp.minimum(scores[v] - top, 0.0)), 0.0))
        total = exps[0]
        for e in exps[1:]:
            total = total + e
        scale = 1.0 / total
        joined = exps[0] * scale * query
        weights_ref[0, :, at] = exps[0] * scale
        for v in range(vehicles):
            weight = exps[v + 1] * scale
            weights_ref[v + 1, :, at] = weight
            joined = joined + weight * enc_ref[v, :, at].astype(F32)
        put_row(taps_ref, r, joined.astype(BF16).astype(F32))

    for h in range(2):
        wide_ref[...] = cot_ref[h].astype(F32)
        for r in range(half):
            at = slice((h * half + r) * LANES, (h * half + r + 1) * LANES)
            cotw_ref[:, at] = wide_ref[pl.ds(r, channels, stride=half), :]

    for j in range(cells // CHUNK):
        at = slice(j * CHUNK, (j + 1) * CHUNK)
        pre = conv_chunk(wt_ref, taps_ref, j)
        sig = sigmoid(pre)
        joined = taps_ref[
            channels : 2 * channels, 2 * LANES + j * CHUNK : 2 * LANES + (j + 1) * CHUNK
        ].astype(F32)
        out_ref[:, at] = joined + pre * sig
        slope = cotw_ref[:, at] * (sig * (1.0 + pre * (1.0 - sig)))
        slope = slope.astype(BF16).astype(F32)
        for k in range(CHUNK // LANES):
            put_row(slope_ref, j * (CHUNK // LANES) + k, slope[:, k * LANES : (k + 1) * LANES])

    for k in range(half):
        at = pl.ds(pl.multiple_of((me * half + k) * LANES, LANES), LANES)
        wide_ref[pl.ds(k, channels, stride=half), :] = out_ref[:, at]
    refined_ref[...] = wide_ref[...].astype(BF16)

    flip_weight(w_ref, wt_ref)
    for j in range(cells // CHUNK):
        at = slice(j * CHUNK, (j + 1) * CHUNK)
        jg_ref[:, at] = conv_chunk(wt_ref, slope_ref, j) + cotw_ref[:, at]

    base = me * half * LANES
    slope_half = slope_ref[
        channels : 2 * channels, pl.ds(pl.multiple_of(base + 2 * LANES, LANES), half * LANES)
    ]
    for a in range(3):
        depth = 3 * channels
        at = pl.ds(pl.multiple_of(base + a * 2 * LANES, LANES), half * LANES)
        grad_ref[a * depth : (a + 1) * depth, :] = dot_nt(taps_ref[:, at], slope_half).astype(BF16)

    acc = jnp.zeros((channels, LANES), F32)
    for r in range(rows):
        at = slice(r * LANES, (r + 1) * LANES)
        query = enc_ref[ego, :, at].astype(F32)
        jg = jg_ref[:, at]
        w_self = weights_ref[0, :, at]
        dot_self = colsum(jg * query)
        mean = w_self * dot_self
        dots = []
        for v in range(vehicles):
            dot = colsum(jg * enc_ref[v, :, at].astype(F32))
            mean = mean + weights_ref[v + 1, :, at] * dot
            dots.append(dot)
        slope_self = w_self * (dot_self - mean)
        ego_sum = slope_self * (2.0 * query + embed)
        for v in range(vehicles):
            slope_v = weights_ref[v + 1, :, at] * (dots[v] - mean)
            weights_ref[8 + v, :, at] = slope_v
            ego_sum = ego_sum + slope_v * enc_ref[v, :, at].astype(F32)
        ego_term = w_self * jg + ego_sum * inv
        for v in range(local):
            veh = me * local + v
            weight_v = weights_ref[veh + 1, :, at]
            slope_v = weights_ref[veh + 8, :, at]
            part = weight_v * jg + (slope_v * inv) * query
            eg_ref[v, :, at] = jnp.where(veh == ego, ego_term, part).astype(BF16)
        mine = jnp.where(me == r // half, inv, 0.0)
        acc = acc + (slope_self * mine) * query
    row = dot_nt(jnp.ones((16, LANES), F32), acc, precision=lax.Precision.HIGHEST)
    grad_ref[9 * channels :, :] = row.astype(BF16)


def post(ids, enc, live, embed, cot, weight, local):
    vehicles, channels, cells = enc.shape
    vm = pl.BlockSpec(memory_space=pltpu.VMEM)
    deep = cot.shape[1]
    return pl.pallas_call(
        post_kernel,
        out_shape=(
            jax.ShapeDtypeStruct((deep, LANES), BF16),
            jax.ShapeDtypeStruct((9 * channels + 16, channels), BF16),
            jax.ShapeDtypeStruct((local, channels, cells), BF16),
        ),
        in_specs=[pl.BlockSpec(memory_space=pltpu.SMEM)] + [vm] * 5,
        out_specs=(vm, vm, vm),
        scratch_shapes=[
            pltpu.VMEM((deep, LANES), F32),
            pltpu.VMEM((channels, cells), F32),
            pltpu.VMEM((3 * channels, cells + 4 * LANES), BF16),
            pltpu.VMEM((3 * channels, cells + 4 * LANES), BF16),
            pltpu.VMEM((channels, 9 * channels), BF16),
            pltpu.VMEM((channels, cells), F32),
            pltpu.VMEM((16, 1, cells), F32),
            pltpu.VMEM((channels, cells), F32),
        ],
        compiler_params=pltpu.CompilerParams(vmem_limit_bytes=VMEM_LIMIT),
        cost_estimate=pl.CostEstimate(
            flops=5 * 9 * channels * channels * cells,
            bytes_accessed=16 * channels * cells,
            transcendentals=channels * cells,
        ),
        name="post",
    )(ids, enc, live, embed, cot, weight)


def back_kernel(
    x_ref, pre_ref, eg_ref, w_ref, fg_ref, grad_ref, wide_ref, taps_ref, slope_ref, wb_ref, acc_ref
):
    channels = w_ref.shape[1]
    cells = pre_ref.shape[-1]
    rows = cells // LANES
    depth = 3 * channels
    first = pl.program_id(0) == 0

    @pl.when(first)
    def _():
        flip_weight(w_ref, wb_ref)
        acc_ref[...] = jnp.zeros_like(acc_ref)

    load_map(x_ref, wide_ref, taps_ref, rows)
    clear_pads(slope_ref, cells)
    for r in range(rows):
        at = slice(r * LANES, (r + 1) * LANES)
        slope = eg_ref[0, :, at].astype(F32) * silu_slope(pre_ref[0, :, at])
        put_row(slope_ref, r, slope.astype(BF16).astype(F32))
    here = slope_ref[channels : 2 * channels, 2 * LANES : 2 * LANES + cells]
    for a in range(3):
        acc_ref[a * depth : (a + 1) * depth, :] += dot_nt(
            taps_ref[:, a * 2 * LANES : a * 2 * LANES + cells], here
        )

    @pl.when(pl.program_id(0) == pl.num_programs(0) - 1)
    def _():
        grad_ref[...] = acc_ref[...].astype(BF16)

    for j in range(cells // CHUNK):
        back = conv_chunk(wb_ref, slope_ref, j)
        for k in range(CHUNK // LANES):
            r = j * (CHUNK // LANES) + k
            fg_ref[0, pl.ds(r, channels, stride=rows), :] = back[
                :, k * LANES : (k + 1) * LANES
            ] + eg_ref[0, :, r * LANES : (r + 1) * LANES].astype(F32)


def back(x, pre, eg, weight):
    veh, channels, cells = pre.shape
    deep = x.shape[1]
    return pl.pallas_call(
        back_kernel,
        grid=(veh,),
        out_shape=(
            jax.ShapeDtypeStruct((veh, deep, LANES), F32),
            jax.ShapeDtypeStruct((9 * channels, channels), BF16),
        ),
        in_specs=[
            pl.BlockSpec((1, deep, LANES), lambda v: (v, 0, 0)),
            pl.BlockSpec((1, channels, cells), lambda v: (v, 0, 0)),
            pl.BlockSpec((1, channels, cells), lambda v: (v, 0, 0)),
            pl.BlockSpec((9 * channels, channels), lambda v: (0, 0)),
        ],
        out_specs=(
            pl.BlockSpec((1, deep, LANES), lambda v: (v, 0, 0)),
            pl.BlockSpec((9 * channels, channels), lambda v: (0, 0)),
        ),
        scratch_shapes=[
            pltpu.VMEM((deep, LANES), F32),
            pltpu.VMEM((3 * channels, cells + 4 * LANES), BF16),
            pltpu.VMEM((3 * channels, cells + 4 * LANES), BF16),
            pltpu.VMEM((channels, 9 * channels), BF16),
            pltpu.VMEM((9 * channels, channels), F32),
        ],
        compiler_params=pltpu.CompilerParams(vmem_limit_bytes=VMEM_LIMIT),
        cost_estimate=pl.CostEstimate(
            flops=4 * veh * 9 * channels * channels * cells,
            bytes_accessed=veh * channels * cells * 12,
            transcendentals=veh * channels * cells,
        ),
        name="back",
    )(x, pre, eg, weight)


def body(
    features, counts, ego_ids, req_tiles, req_count, ego_embed, enc_weight, post_weight, cotangent
):
    batch, local, channels, rows, breadth = features.shape
    me = lax.axis_index("veh")
    veh_here = me * local + jnp.arange(local)
    present = (veh_here < counts[0]) & (veh_here != ego_ids[0])
    live_count = jnp.where(present, req_count[0], 0)
    asked = (req_tiles[0][:, :, None] == (jnp.arange(breadth) // TILE)[None, None, :]) & (
        jnp.arange(KMAX)[None, :, None] < live_count[:, None, None]
    )
    live = jnp.sum(asked.astype(F32), axis=1)
    live = lax.all_gather(live, "veh", axis=0, tiled=True)
    half = cotangent.shape[2]
    cot = lax.all_gather(cotangent.reshape(1, channels * half, breadth), "veh", axis=0, tiled=True)
    x = features.reshape(local, channels * rows, breadth)
    enc_w = enc_weight.reshape(9 * channels, channels)
    post_w = post_weight.reshape(9 * channels, channels)
    pre, encoded = encode(x, enc_w)
    enc_all = lax.all_gather(encoded, "veh", axis=0, tiled=True)
    ids = jnp.stack([ego_ids[0], me]).astype(jnp.int32)
    embed = jnp.broadcast_to(ego_embed.astype(F32)[:, None], (channels, LANES))
    refined, post_part, eg = post(ids, enc_all, live, embed, cot, post_w, local)
    post_sum = lax.psum(post_part, ("scene", "veh")).astype(F32)
    fg, enc_part = back(x, pre, eg, enc_w)
    enc_sum = lax.psum(enc_part, ("scene", "veh")).astype(F32)
    return (
        refined.reshape(batch, channels, half, breadth),
        fg.reshape(features.shape),
        enc_sum.reshape(enc_weight.shape),
        post_sum[: 9 * channels].reshape(post_weight.shape),
        post_sum[9 * channels],
    )


def solution(mesh):
    in_specs = (
        P("scene", "veh", None, None, None),
        P("scene"),
        P("scene"),
        P("scene", "veh", None),
        P("scene", "veh"),
        P(),
        P(),
        P(),
        P("scene", None, "veh", None),
    )
    out_specs = (P("scene", None, "veh", None), P("scene", "veh", None, None, None), P(), P(), P())
    return jax.shard_map(body, mesh=mesh, in_specs=in_specs, out_specs=out_specs, check_vma=False)
```

```python
import jax
import jax.numpy as jnp
from jax import lax
from jax.experimental import pallas as pl
from jax.experimental.pallas import tpu as pltpu
from jax.sharding import PartitionSpec as P

TILE = 32
KMAX = 2
F32 = jnp.float32
BF16 = jnp.bfloat16
LANES = 128
CHUNK = 512
VMEM_LIMIT = 56 * 1024 * 1024


def sigmoid(z):
    return 1.0 / (1.0 + jnp.exp(-z))


def silu_slope(z):
    sig = sigmoid(z)
    return sig * (1.0 + z * (1.0 - sig))


def clear_pads(taps_ref, cells):
    rows = taps_ref.shape[0]
    taps_ref[:, : 2 * LANES] = jnp.zeros((rows, 2 * LANES), BF16)
    taps_ref[:, 2 * LANES + cells :] = jnp.zeros((rows, 2 * LANES), BF16)


def put_row(taps_ref, r, row):
    channels = row.shape[0]
    lane = lax.broadcasted_iota(jnp.int32, row.shape, 1)
    at = slice((r + 2) * LANES, (r + 3) * LANES)
    left = jnp.where(lane >= 2, pltpu.roll(row, 2, 1), 0.0)
    right = jnp.where(lane < LANES - 2, pltpu.roll(row, LANES - 2, 1), 0.0)
    taps_ref[:channels, at] = left.astype(BF16)
    taps_ref[channels : 2 * channels, at] = row.astype(BF16)
    taps_ref[2 * channels :, at] = right.astype(BF16)


def turn_weight(w_ref, wt_ref):
    channels = w_ref.shape[1]
    for t in range(9):
        at = slice(t * channels, (t + 1) * channels)
        wt_ref[:, at] = w_ref[at, :].T


def flip_weight(w_ref, wb_ref):
    channels = w_ref.shape[1]
    for t in range(9):
        wb_ref[:, t * channels : (t + 1) * channels] = w_ref[
            (8 - t) * channels : (9 - t) * channels, :
        ]


def conv_chunk(w_ref, taps_ref, j):
    depth = taps_ref.shape[0]
    total = None
    for a in range(3):
        part = jnp.dot(
            w_ref[:, a * depth : (a + 1) * depth],
            taps_ref[:, a * 2 * LANES + j * CHUNK : a * 2 * LANES + (j + 1) * CHUNK],
            preferred_element_type=F32,
        )
        total = part if total is None else total + part
    return total


def dot_nt(left, right, precision=None):
    return lax.dot_general(
        left, right, (((1,), (1,)), ((), ())), preferred_element_type=F32, precision=precision
    )


def load_map(x_ref, wide_ref, taps_ref, rows):
    channels = taps_ref.shape[0] // 3
    wide_ref[...] = x_ref[0].astype(F32)
    clear_pads(taps_ref, rows * LANES)
    for r in range(rows):
        put_row(taps_ref, r, wide_ref[pl.ds(r, channels, stride=rows), :])


def encode_kernel(x_ref, w_ref, pre_ref, enc_ref, wide_ref, taps_ref, wt_ref):
    channels = w_ref.shape[1]
    cells = pre_ref.shape[-1]
    rows = cells // LANES

    @pl.when(pl.program_id(0) == 0)
    def _():
        turn_weight(w_ref, wt_ref)

    load_map(x_ref, wide_ref, taps_ref, rows)
    for j in range(cells // CHUNK):
        at = slice(j * CHUNK, (j + 1) * CHUNK)
        pre = conv_chunk(wt_ref, taps_ref, j)
        here = taps_ref[channels : 2 * channels, 2 * LANES + j * CHUNK : 2 * LANES + (j + 1) * CHUNK]
        pre_ref[0, :, at] = pre
        enc_ref[0, :, at] = (here.astype(F32) + pre * sigmoid(pre)).astype(BF16)


def encode(x, weight):
    veh, deep, _ = x.shape
    channels = weight.shape[1]
    cells = deep // channels * LANES
    return pl.pallas_call(
        encode_kernel,
        grid=(veh,),
        out_shape=(
            jax.ShapeDtypeStruct((veh, channels, cells), F32),
            jax.ShapeDtypeStruct((veh, channels, cells), BF16),
        ),
        in_specs=[
            pl.BlockSpec((1, deep, LANES), lambda v: (v, 0, 0)),
            pl.BlockSpec((9 * channels, channels), lambda v: (0, 0)),
        ],
        out_specs=(
            pl.BlockSpec((1, channels, cells), lambda v: (v, 0, 0)),
            pl.BlockSpec((1, channels, cells), lambda v: (v, 0, 0)),
        ),
        scratch_shapes=[
            pltpu.VMEM((deep, LANES), F32),
            pltpu.VMEM((3 * channels, cells + 4 * LANES), BF16),
            pltpu.VMEM((channels, 9 * channels), BF16),
        ],
        compiler_params=pltpu.CompilerParams(vmem_limit_bytes=VMEM_LIMIT),
        cost_estimate=pl.CostEstimate(
            flops=2 * veh * 9 * channels * channels * cells,
            bytes_accessed=veh * channels * cells * 8,
            transcendentals=veh * channels * cells,
        ),
        name="encode",
    )(x, weight)


def post_kernel(
    ids_ref, enc_ref, live_ref, embed_ref, cot_ref, w_ref,
    refined_ref, grad_ref, eg_ref,
    wide_ref, cotw_ref, taps_ref, slope_ref, wt_ref, out_ref, weights_ref, jg_ref,
):
    vehicles, channels, cells = enc_ref.shape
    rows = cells // LANES
    half = rows // 2
    local = eg_ref.shape[0]
    ego, me = ids_ref[0], ids_ref[1]
    inv = 1.0 / channels
    turn_weight(w_ref, wt_ref)
    clear_pads(taps_ref, cells)
    clear_pads(slope_ref, cells)
    embed = embed_ref[...]

    def colsum(x):
        return jnp.sum(x, axis=0, keepdims=True)

    for r in range(rows):
        at = slice(r * LANES, (r + 1) * LANES)
        query = enc_ref[ego, :, at].astype(F32)
        score_self = colsum(query * (query + embed)) * inv
        scores, top = [], score_self
        for v in range(vehicles):
            score = colsum(query * enc_ref[v, :, at].astype(F32)) * inv
            live = live_ref[v : v + 1, :] > 0.5
            top = jnp.maximum(top, jnp.where(live, score, -jnp.inf))
            scores.append(score)
        exps = [jnp.exp(score_self - top)]
        for v in range(vehicles):
            live = live_ref[v : v + 1, :] > 0.5
            exps.append(jnp.where(live, jnp.exp(jnp.minimum(scores[v] - top, 0.0)), 0.0))
        total = exps[0]
        for e in exps[1:]:
            total = total + e
        scale = 1.0 / total
        joined = exps[0] * scale * query
        weights_ref[0, :, at] = exps[0] * scale
        for v in range(vehicles):
            weight = exps[v + 1] * scale
            weights_ref[v + 1, :, at] = weight
            joined = joined + weight * enc_ref[v, :, at].astype(F32)
        put_row(taps_ref, r, joined.astype(BF16).astype(F32))

    for h in range(2):
        wide_ref[...] = cot_ref[h].astype(F32)
        for r in range(half):
            at = slice((h * half + r) * LANES, (h * half + r + 1) * LANES)
            cotw_ref[:, at] = wide_ref[pl.ds(r, channels, stride=half), :]

    for j in range(cells // CHUNK):
        at = slice(j * CHUNK, (j + 1) * CHUNK)
        pre = conv_chunk(wt_ref, taps_ref, j)
        sig = sigmoid(pre)
        joined = taps_ref[
            channels : 2 * channels, 2 * LANES + j * CHUNK : 2 * LANES + (j + 1) * CHUNK
        ].astype(F32)
        out_ref[:, at] = joined + pre * sig
        slope = cotw_ref[:, at] * (sig * (1.0 + pre * (1.0 - sig)))
        slope = slope.astype(BF16).astype(F32)
        for k in range(CHUNK // LANES):
            put_row(slope_ref, j * (CHUNK // LANES) + k, slope[:, k * LANES : (k + 1) * LANES])

    for k in range(half):
        at = pl.ds(pl.multiple_of((me * half + k) * LANES, LANES), LANES)
        wide_ref[pl.ds(k, channels, stride=half), :] = out_ref[:, at]
    refined_ref[...] = wide_ref[...].astype(BF16)

    flip_weight(w_ref, wt_ref)
    for j in range(cells // CHUNK):
        at = slice(j * CHUNK, (j + 1) * CHUNK)
        jg_ref[:, at] = conv_chunk(wt_ref, slope_ref, j) + cotw_ref[:, at]

    base = me * half * LANES
    slope_half = slope_ref[
        channels : 2 * channels, pl.ds(pl.multiple_of(base + 2 * LANES, LANES), half * LANES)
    ]
    for a in range(3):
        depth = 3 * channels
        at = pl.ds(pl.multiple_of(base + a * 2 * LANES, LANES), half * LANES)
        grad_ref[a * depth : (a + 1) * depth, :] = dot_nt(taps_ref[:, at], slope_half).astype(BF16)

    acc = jnp.zeros((channels, LANES), F32)
    for r in range(rows):
        at = slice(r * LANES, (r + 1) * LANES)
        query = enc_ref[ego, :, at].astype(F32)
        jg = jg_ref[:, at]
        w_self = weights_ref[0, :, at]
        dot_self = colsum(jg * query)
        mean = w_self * dot_self
        dots = []
        for v in range(vehicles):
            dot = colsum(jg * enc_ref[v, :, at].astype(F32))
            mean = mean + weights_ref[v + 1, :, at] * dot
            dots.append(dot)
        slope_self = w_self * (dot_self - mean)
        ego_sum = slope_self * (2.0 * query + embed)
        for v in range(vehicles):
            slope_v = weights_ref[v + 1, :, at] * (dots[v] - mean)
            weights_ref[8 + v, :, at] = slope_v
            ego_sum = ego_sum + slope_v * enc_ref[v, :, at].astype(F32)
        ego_term = w_self * jg + ego_sum * inv
        for v in range(local):
            veh = me * local + v
            weight_v = weights_ref[veh + 1, :, at]
            slope_v = weights_ref[veh + 8, :, at]
            part = weight_v * jg + (slope_v * inv) * query
            eg_ref[v, :, at] = jnp.where(veh == ego, ego_term, part).astype(BF16)
        mine = jnp.where(me == r // half, inv, 0.0)
        acc = acc + (slope_self * mine) * query
    row = dot_nt(jnp.ones((16, LANES), F32), acc, precision=lax.Precision.HIGHEST)
    grad_ref[9 * channels :, :] = row.astype(BF16)


def post(ids, enc, live, embed, cot, weight, local):
    vehicles, channels, cells = enc.shape
    vm = pl.BlockSpec(memory_space=pltpu.VMEM)
    deep = cot.shape[1]
    return pl.pallas_call(
        post_kernel,
        out_shape=(
            jax.ShapeDtypeStruct((deep, LANES), BF16),
            jax.ShapeDtypeStruct((9 * channels + 16, channels), BF16),
            jax.ShapeDtypeStruct((local, channels, cells), BF16),
        ),
        in_specs=[pl.BlockSpec(memory_space=pltpu.SMEM)] + [vm] * 5,
        out_specs=(vm, vm, vm),
        scratch_shapes=[
            pltpu.VMEM((deep, LANES), F32),
            pltpu.VMEM((channels, cells), F32),
            pltpu.VMEM((3 * channels, cells + 4 * LANES), BF16),
            pltpu.VMEM((3 * channels, cells + 4 * LANES), BF16),
            pltpu.VMEM((channels, 9 * channels), BF16),
            pltpu.VMEM((channels, cells), F32),
            pltpu.VMEM((16, 1, cells), F32),
            pltpu.VMEM((channels, cells), F32),
        ],
        compiler_params=pltpu.CompilerParams(vmem_limit_bytes=VMEM_LIMIT),
        cost_estimate=pl.CostEstimate(
            flops=5 * 9 * channels * channels * cells,
            bytes_accessed=16 * channels * cells,
            transcendentals=channels * cells,
        ),
        name="post",
    )(ids, enc, live, embed, cot, weight)


def back_kernel(
    x_ref, pre_ref, eg_ref, w_ref, fg_ref, grad_ref, wide_ref, taps_ref, slope_ref, wb_ref, acc_ref
):
    channels = w_ref.shape[1]
    cells = pre_ref.shape[-1]
    rows = cells // LANES
    depth = 3 * channels
    first = pl.program_id(0) == 0

    @pl.when(first)
    def _():
        flip_weight(w_ref, wb_ref)
        acc_ref[...] = jnp.zeros_like(acc_ref)

    load_map(x_ref, wide_ref, taps_ref, rows)
    clear_pads(slope_ref, cells)
    for r in range(rows):
        at = slice(r * LANES, (r + 1) * LANES)
        slope = eg_ref[0, :, at].astype(F32) * silu_slope(pre_ref[0, :, at])
        put_row(slope_ref, r, slope.astype(BF16).astype(F32))
    here = slope_ref[channels : 2 * channels, 2 * LANES : 2 * LANES + cells]
    for a in range(3):
        acc_ref[a * depth : (a + 1) * depth, :] += dot_nt(
            taps_ref[:, a * 2 * LANES : a * 2 * LANES + cells], here
        )

    @pl.when(pl.program_id(0) == pl.num_programs(0) - 1)
    def _():
        grad_ref[...] = acc_ref[...].astype(BF16)

    for j in range(cells // CHUNK):
        back = conv_chunk(wb_ref, slope_ref, j)
        for k in range(CHUNK // LANES):
            r = j * (CHUNK // LANES) + k
            fg_ref[0, pl.ds(r, channels, stride=rows), :] = back[
                :, k * LANES : (k + 1) * LANES
            ] + eg_ref[0, :, r * LANES : (r + 1) * LANES].astype(F32)


def back(x, pre, eg, weight):
    veh, channels, cells = pre.shape
    deep = x.shape[1]
    return pl.pallas_call(
        back_kernel,
        grid=(veh,),
        out_shape=(
            jax.ShapeDtypeStruct((veh, deep, LANES), F32),
            jax.ShapeDtypeStruct((9 * channels, channels), BF16),
        ),
        in_specs=[
            pl.BlockSpec((1, deep, LANES), lambda v: (v, 0, 0)),
            pl.BlockSpec((1, channels, cells), lambda v: (v, 0, 0)),
            pl.BlockSpec((1, channels, cells), lambda v: (v, 0, 0)),
            pl.BlockSpec((9 * channels, channels), lambda v: (0, 0)),
        ],
        out_specs=(
            pl.BlockSpec((1, deep, LANES), lambda v: (v, 0, 0)),
            pl.BlockSpec((9 * channels, channels), lambda v: (0, 0)),
        ),
        scratch_shapes=[
            pltpu.VMEM((deep, LANES), F32),
            pltpu.VMEM((3 * channels, cells + 4 * LANES), BF16),
            pltpu.VMEM((3 * channels, cells + 4 * LANES), BF16),
            pltpu.VMEM((channels, 9 * channels), BF16),
            pltpu.VMEM((9 * channels, channels), F32),
        ],
        compiler_params=pltpu.CompilerParams(vmem_limit_bytes=VMEM_LIMIT),
        cost_estimate=pl.CostEstimate(
            flops=4 * veh * 9 * channels * channels * cells,
            bytes_accessed=veh * channels * cells * 12,
            transcendentals=veh * channels * cells,
        ),
        name="back",
    )(x, pre, eg, weight)


def swap(x, axis, bit):
    size = lax.axis_size(axis)
    return lax.ppermute(x, axis, [(i, i ^ (1 << bit)) for i in range(size)])


def sum_over_devices(part, order):
    pad = -part.shape[0] % (1 << len(order))
    total = jnp.pad(part, ((0, pad), (0, 0))).astype(F32)
    for axis, bit in order:
        half = total.shape[0] // 2
        high = ((lax.axis_index(axis) >> bit) & 1) == 1
        low_rows, high_rows = total[:half], total[half:]
        sent = jnp.where(high, low_rows, high_rows).astype(BF16)
        total = jnp.where(high, high_rows, low_rows) + swap(sent, axis, bit).astype(F32)
    whole = total.astype(BF16)
    for axis, bit in reversed(order):
        high = ((lax.axis_index(axis) >> bit) & 1) == 1
        other = swap(whole, axis, bit)
        whole = jnp.concatenate([jnp.where(high, other, whole), jnp.where(high, whole, other)], axis=0)
    return whole[: part.shape[0]].astype(F32)


def body(
    features, counts, ego_ids, req_tiles, req_count, ego_embed, enc_weight, post_weight, cotangent
):
    batch, local, channels, rows, breadth = features.shape
    me = lax.axis_index("veh")
    veh_here = me * local + jnp.arange(local)
    present = (veh_here < counts[0]) & (veh_here != ego_ids[0])
    live_count = jnp.where(present, req_count[0], 0)
    asked = (req_tiles[0][:, :, None] == (jnp.arange(breadth) // TILE)[None, None, :]) & (
        jnp.arange(KMAX)[None, :, None] < live_count[:, None, None]
    )
    live = jnp.sum(asked.astype(F32), axis=1)
    live = lax.all_gather(live, "veh", axis=0, tiled=True)
    half = cotangent.shape[2]
    cot = lax.all_gather(cotangent.reshape(1, channels * half, breadth), "veh", axis=0, tiled=True)
    x = features.reshape(local, channels * rows, breadth)
    enc_w = enc_weight.reshape(9 * channels, channels)
    post_w = post_weight.reshape(9 * channels, channels)
    pre, encoded = encode(x, enc_w)
    enc_all = lax.all_gather(encoded, "veh", axis=0, tiled=True)
    ids = jnp.stack([ego_ids[0], me]).astype(jnp.int32)
    embed = jnp.broadcast_to(ego_embed.astype(F32)[:, None], (channels, LANES))
    refined, post_part, eg = post(ids, enc_all, live, embed, cot, post_w, local)
    scene_bits = [("scene", b) for b in range(lax.axis_size("scene").bit_length() - 1)]
    veh_bits = [("veh", b) for b in range(lax.axis_size("veh").bit_length() - 1)]
    one = veh_bits + scene_bits
    two = veh_bits + scene_bits[1:2] + scene_bits[:1] + scene_bits[2:]
    post_sum = sum_over_devices(post_part, two)
    fg, enc_part = back(x, pre, eg, enc_w)
    cut = enc_part.shape[0] // 2
    enc_sum = jnp.concatenate(
        [sum_over_devices(enc_part[:cut], one), sum_over_devices(enc_part[cut:], two)], axis=0
    )
    return (
        refined.reshape(batch, channels, half, breadth),
        fg.reshape(features.shape),
        enc_sum.reshape(enc_weight.shape),
        post_sum[: 9 * channels].reshape(post_weight.shape),
        post_sum[9 * channels],
    )


def solution(mesh):
    in_specs = (
        P("scene", "veh", None, None, None),
        P("scene"),
        P("scene"),
        P("scene", "veh", None),
        P("scene", "veh"),
        P(),
        P(),
        P(),
        P("scene", None, "veh", None),
    )
    out_specs = (P("scene", None, "veh", None), P("scene", "veh", None, None, None), P(), P(), P())
    return jax.shard_map(body, mesh=mesh, in_specs=in_specs, out_specs=out_specs, check_vma=False)
```

```python
import jax
import jax.numpy as jnp
from jax import lax
from jax.experimental import pallas as pl
from jax.experimental.pallas import tpu as pltpu
from jax.sharding import PartitionSpec as P

TILE = 32
KMAX = 2
F32 = jnp.float32
BF16 = jnp.bfloat16
LANES = 128
CHUNK = 512
VMEM_LIMIT = 56 * 1024 * 1024


def sigmoid(z):
    return 1.0 / (1.0 + jnp.exp(-z))


def silu_slope(z):
    sig = sigmoid(z)
    return sig * (1.0 + z * (1.0 - sig))


def clear_pads(taps_ref, cells):
    rows = taps_ref.shape[0]
    taps_ref[:, : 2 * LANES] = jnp.zeros((rows, 2 * LANES), BF16)
    taps_ref[:, 2 * LANES + cells :] = jnp.zeros((rows, 2 * LANES), BF16)


def put_row(taps_ref, r, row):
    channels = row.shape[0]
    lane = lax.broadcasted_iota(jnp.int32, row.shape, 1)
    at = slice((r + 2) * LANES, (r + 3) * LANES)
    left = jnp.where(lane >= 2, pltpu.roll(row, 2, 1), 0.0)
    right = jnp.where(lane < LANES - 2, pltpu.roll(row, LANES - 2, 1), 0.0)
    taps_ref[:channels, at] = left.astype(BF16)
    taps_ref[channels : 2 * channels, at] = row.astype(BF16)
    taps_ref[2 * channels :, at] = right.astype(BF16)


def turn_weight(w_ref, wt_ref):
    channels = w_ref.shape[1]
    for t in range(9):
        at = slice(t * channels, (t + 1) * channels)
        wt_ref[:, at] = w_ref[at, :].T


def flip_weight(w_ref, wb_ref):
    channels = w_ref.shape[1]
    for t in range(9):
        wb_ref[:, t * channels : (t + 1) * channels] = w_ref[
            (8 - t) * channels : (9 - t) * channels, :
        ]


def conv_chunk(w_ref, taps_ref, j):
    depth = taps_ref.shape[0]
    total = None
    for a in range(3):
        part = jnp.dot(
            w_ref[:, a * depth : (a + 1) * depth],
            taps_ref[:, a * 2 * LANES + j * CHUNK : a * 2 * LANES + (j + 1) * CHUNK],
            preferred_element_type=F32,
        )
        total = part if total is None else total + part
    return total


def dot_nt(left, right, precision=None):
    return lax.dot_general(
        left, right, (((1,), (1,)), ((), ())), preferred_element_type=F32, precision=precision
    )


def load_map(x_ref, wide_ref, taps_ref, rows):
    channels = taps_ref.shape[0] // 3
    wide_ref[...] = x_ref[0].astype(F32)
    clear_pads(taps_ref, rows * LANES)
    for r in range(rows):
        put_row(taps_ref, r, wide_ref[pl.ds(r, channels, stride=rows), :])


def encode_kernel(x_ref, w_ref, pre_ref, enc_ref, wide_ref, taps_ref, wt_ref):
    channels = w_ref.shape[1]
    cells = pre_ref.shape[-1]
    rows = cells // LANES

    @pl.when(pl.program_id(0) == 0)
    def _():
        turn_weight(w_ref, wt_ref)

    load_map(x_ref, wide_ref, taps_ref, rows)
    for j in range(cells // CHUNK):
        at = slice(j * CHUNK, (j + 1) * CHUNK)
        pre = conv_chunk(wt_ref, taps_ref, j)
        here = taps_ref[channels : 2 * channels, 2 * LANES + j * CHUNK : 2 * LANES + (j + 1) * CHUNK]
        pre_ref[0, :, at] = pre
        enc_ref[0, :, at] = (here.astype(F32) + pre * sigmoid(pre)).astype(BF16)


def encode(x, weight):
    veh, deep, _ = x.shape
    channels = weight.shape[1]
    cells = deep // channels * LANES
    return pl.pallas_call(
        encode_kernel,
        grid=(veh,),
        out_shape=(
            jax.ShapeDtypeStruct((veh, channels, cells), F32),
            jax.ShapeDtypeStruct((veh, channels, cells), BF16),
        ),
        in_specs=[
            pl.BlockSpec((1, deep, LANES), lambda v: (v, 0, 0)),
            pl.BlockSpec((9 * channels, channels), lambda v: (0, 0)),
        ],
        out_specs=(
            pl.BlockSpec((1, channels, cells), lambda v: (v, 0, 0)),
            pl.BlockSpec((1, channels, cells), lambda v: (v, 0, 0)),
        ),
        scratch_shapes=[
            pltpu.VMEM((deep, LANES), F32),
            pltpu.VMEM((3 * channels, cells + 4 * LANES), BF16),
            pltpu.VMEM((channels, 9 * channels), BF16),
        ],
        compiler_params=pltpu.CompilerParams(vmem_limit_bytes=VMEM_LIMIT),
        cost_estimate=pl.CostEstimate(
            flops=2 * veh * 9 * channels * channels * cells,
            bytes_accessed=veh * channels * cells * 8,
            transcendentals=veh * channels * cells,
        ),
        name="encode",
    )(x, weight)


def post_kernel(
    ids_ref, enc_ref, live_ref, embed_ref, cot_ref, w_ref,
    refined_ref, grad_ref, eg_ref,
    wide_ref, cotw_ref, taps_ref, slope_ref, wt_ref, out_ref, weights_ref, jg_ref,
):
    vehicles, channels, cells = enc_ref.shape
    rows = cells // LANES
    half = rows // 2
    local = eg_ref.shape[0]
    ego, me = ids_ref[0], ids_ref[1]
    inv = 1.0 / channels
    turn_weight(w_ref, wt_ref)
    clear_pads(taps_ref, cells)
    clear_pads(slope_ref, cells)
    embed = embed_ref[...]

    def colsum(x):
        return jnp.sum(x, axis=0, keepdims=True)

    for r in range(rows):
        at = slice(r * LANES, (r + 1) * LANES)
        query = enc_ref[ego, :, at].astype(F32)
        score_self = colsum(query * (query + embed)) * inv
        scores, top = [], score_self
        for v in range(vehicles):
            score = colsum(query * enc_ref[v, :, at].astype(F32)) * inv
            live = live_ref[v : v + 1, :] > 0.5
            top = jnp.maximum(top, jnp.where(live, score, -jnp.inf))
            scores.append(score)
        exps = [jnp.exp(score_self - top)]
        for v in range(vehicles):
            live = live_ref[v : v + 1, :] > 0.5
            exps.append(jnp.where(live, jnp.exp(jnp.minimum(scores[v] - top, 0.0)), 0.0))
        total = exps[0]
        for e in exps[1:]:
            total = total + e
        scale = 1.0 / total
        joined = exps[0] * scale * query
        weights_ref[0, :, at] = exps[0] * scale
        for v in range(vehicles):
            weight = exps[v + 1] * scale
            weights_ref[v + 1, :, at] = weight
            joined = joined + weight * enc_ref[v, :, at].astype(F32)
        put_row(taps_ref, r, joined.astype(BF16).astype(F32))

    for h in range(2):
        wide_ref[...] = cot_ref[h].astype(F32)
        for r in range(half):
            at = slice((h * half + r) * LANES, (h * half + r + 1) * LANES)
            cotw_ref[:, at] = wide_ref[pl.ds(r, channels, stride=half), :]

    for j in range(cells // CHUNK):
        at = slice(j * CHUNK, (j + 1) * CHUNK)
        pre = conv_chunk(wt_ref, taps_ref, j)
        sig = sigmoid(pre)
        joined = taps_ref[
            channels : 2 * channels, 2 * LANES + j * CHUNK : 2 * LANES + (j + 1) * CHUNK
        ].astype(F32)
        out_ref[:, at] = joined + pre * sig
        slope = cotw_ref[:, at] * (sig * (1.0 + pre * (1.0 - sig)))
        slope = slope.astype(BF16).astype(F32)
        for k in range(CHUNK // LANES):
            put_row(slope_ref, j * (CHUNK // LANES) + k, slope[:, k * LANES : (k + 1) * LANES])

    for k in range(half):
        at = pl.ds(pl.multiple_of((me * half + k) * LANES, LANES), LANES)
        wide_ref[pl.ds(k, channels, stride=half), :] = out_ref[:, at]
    refined_ref[...] = wide_ref[...].astype(BF16)

    flip_weight(w_ref, wt_ref)
    for j in range(cells // CHUNK):
        at = slice(j * CHUNK, (j + 1) * CHUNK)
        jg_ref[:, at] = conv_chunk(wt_ref, slope_ref, j) + cotw_ref[:, at]

    base = me * half * LANES
    slope_half = slope_ref[
        channels : 2 * channels, pl.ds(pl.multiple_of(base + 2 * LANES, LANES), half * LANES)
    ]
    for a in range(3):
        depth = 3 * channels
        at = pl.ds(pl.multiple_of(base + a * 2 * LANES, LANES), half * LANES)
        grad_ref[a * depth : (a + 1) * depth, :] = dot_nt(taps_ref[:, at], slope_half).astype(BF16)

    acc = jnp.zeros((channels, LANES), F32)
    for r in range(rows):
        at = slice(r * LANES, (r + 1) * LANES)
        query = enc_ref[ego, :, at].astype(F32)
        jg = jg_ref[:, at]
        w_self = weights_ref[0, :, at]
        dot_self = colsum(jg * query)
        mean = w_self * dot_self
        dots = []
        for v in range(vehicles):
            dot = colsum(jg * enc_ref[v, :, at].astype(F32))
            mean = mean + weights_ref[v + 1, :, at] * dot
            dots.append(dot)
        slope_self = w_self * (dot_self - mean)
        ego_sum = slope_self * (2.0 * query + embed)
        for v in range(vehicles):
            slope_v = weights_ref[v + 1, :, at] * (dots[v] - mean)
            weights_ref[8 + v, :, at] = slope_v
            ego_sum = ego_sum + slope_v * enc_ref[v, :, at].astype(F32)
        ego_term = w_self * jg + ego_sum * inv
        for v in range(local):
            veh = me * local + v
            weight_v = weights_ref[veh + 1, :, at]
            slope_v = weights_ref[veh + 8, :, at]
            part = weight_v * jg + (slope_v * inv) * query
            eg_ref[v, :, at] = jnp.where(veh == ego, ego_term, part).astype(BF16)
        mine = jnp.where(me == r // half, inv, 0.0)
        acc = acc + (slope_self * mine) * query
    row = dot_nt(jnp.ones((16, LANES), F32), acc, precision=lax.Precision.HIGHEST)
    grad_ref[9 * channels :, :] = row.astype(BF16)


def post(ids, enc, live, embed, cot, weight, local):
    vehicles, channels, cells = enc.shape
    vm = pl.BlockSpec(memory_space=pltpu.VMEM)
    deep = cot.shape[1]
    return pl.pallas_call(
        post_kernel,
        out_shape=(
            jax.ShapeDtypeStruct((deep, LANES), BF16),
            jax.ShapeDtypeStruct((9 * channels + 16, channels), BF16),
            jax.ShapeDtypeStruct((local, channels, cells), BF16),
        ),
        in_specs=[pl.BlockSpec(memory_space=pltpu.SMEM)] + [vm] * 5,
        out_specs=(vm, vm, vm),
        scratch_shapes=[
            pltpu.VMEM((deep, LANES), F32),
            pltpu.VMEM((channels, cells), F32),
            pltpu.VMEM((3 * channels, cells + 4 * LANES), BF16),
            pltpu.VMEM((3 * channels, cells + 4 * LANES), BF16),
            pltpu.VMEM((channels, 9 * channels), BF16),
            pltpu.VMEM((channels, cells), F32),
            pltpu.VMEM((16, 1, cells), F32),
            pltpu.VMEM((channels, cells), F32),
        ],
        compiler_params=pltpu.CompilerParams(vmem_limit_bytes=VMEM_LIMIT),
        cost_estimate=pl.CostEstimate(
            flops=5 * 9 * channels * channels * cells,
            bytes_accessed=16 * channels * cells,
            transcendentals=channels * cells,
        ),
        name="post",
    )(ids, enc, live, embed, cot, weight)


def back_kernel(
    x_ref, pre_ref, eg_ref, w_ref, fg_ref, grad_ref, wide_ref, taps_ref, slope_ref, wb_ref, acc_ref
):
    channels = w_ref.shape[1]
    cells = pre_ref.shape[-1]
    rows = cells // LANES
    depth = 3 * channels
    first = pl.program_id(0) == 0

    @pl.when(first)
    def _():
        flip_weight(w_ref, wb_ref)
        acc_ref[...] = jnp.zeros_like(acc_ref)

    load_map(x_ref, wide_ref, taps_ref, rows)
    clear_pads(slope_ref, cells)
    for r in range(rows):
        at = slice(r * LANES, (r + 1) * LANES)
        slope = eg_ref[0, :, at].astype(F32) * silu_slope(pre_ref[0, :, at])
        put_row(slope_ref, r, slope.astype(BF16).astype(F32))
    here = slope_ref[channels : 2 * channels, 2 * LANES : 2 * LANES + cells]
    for a in range(3):
        acc_ref[a * depth : (a + 1) * depth, :] += dot_nt(
            taps_ref[:, a * 2 * LANES : a * 2 * LANES + cells], here
        )

    @pl.when(pl.program_id(0) == pl.num_programs(0) - 1)
    def _():
        grad_ref[...] = acc_ref[...].astype(BF16)

    for j in range(cells // CHUNK):
        back = conv_chunk(wb_ref, slope_ref, j)
        for k in range(CHUNK // LANES):
            r = j * (CHUNK // LANES) + k
            fg_ref[0, pl.ds(r, channels, stride=rows), :] = back[
                :, k * LANES : (k + 1) * LANES
            ] + eg_ref[0, :, r * LANES : (r + 1) * LANES].astype(F32)


def back(x, pre, eg, weight):
    veh, channels, cells = pre.shape
    deep = x.shape[1]
    return pl.pallas_call(
        back_kernel,
        grid=(veh,),
        out_shape=(
            jax.ShapeDtypeStruct((veh, deep, LANES), F32),
            jax.ShapeDtypeStruct((9 * channels, channels), BF16),
        ),
        in_specs=[
            pl.BlockSpec((1, deep, LANES), lambda v: (v, 0, 0)),
            pl.BlockSpec((1, channels, cells), lambda v: (v, 0, 0)),
            pl.BlockSpec((1, channels, cells), lambda v: (v, 0, 0)),
            pl.BlockSpec((9 * channels, channels), lambda v: (0, 0)),
        ],
        out_specs=(
            pl.BlockSpec((1, deep, LANES), lambda v: (v, 0, 0)),
            pl.BlockSpec((9 * channels, channels), lambda v: (0, 0)),
        ),
        scratch_shapes=[
            pltpu.VMEM((deep, LANES), F32),
            pltpu.VMEM((3 * channels, cells + 4 * LANES), BF16),
            pltpu.VMEM((3 * channels, cells + 4 * LANES), BF16),
            pltpu.VMEM((channels, 9 * channels), BF16),
            pltpu.VMEM((9 * channels, channels), F32),
        ],
        compiler_params=pltpu.CompilerParams(vmem_limit_bytes=VMEM_LIMIT),
        cost_estimate=pl.CostEstimate(
            flops=4 * veh * 9 * channels * channels * cells,
            bytes_accessed=veh * channels * cells * 12,
            transcendentals=veh * channels * cells,
        ),
        name="back",
    )(x, pre, eg, weight)


def swap(x, axis, bit):
    size = lax.axis_size(axis)
    return lax.ppermute(x, axis, [(i, i ^ (1 << bit)) for i in range(size)])


def sum_over_devices(part, order):
    pad = -part.shape[0] % (1 << len(order))
    total = jnp.pad(part, ((0, pad), (0, 0))).astype(F32)
    for axis, bit in order:
        half = total.shape[0] // 2
        high = ((lax.axis_index(axis) >> bit) & 1) == 1
        low_rows, high_rows = total[:half], total[half:]
        sent = jnp.where(high, low_rows, high_rows).astype(BF16)
        total = jnp.where(high, high_rows, low_rows) + swap(sent, axis, bit).astype(F32)
    whole = total.astype(BF16)
    for axis, bit in reversed(order):
        high = ((lax.axis_index(axis) >> bit) & 1) == 1
        other = swap(whole, axis, bit)
        whole = jnp.concatenate([jnp.where(high, other, whole), jnp.where(high, whole, other)], axis=0)
    return whole[: part.shape[0]].astype(F32)


def body(
    features, counts, ego_ids, req_tiles, req_count, ego_embed, enc_weight, post_weight, cotangent
):
    batch, local, channels, rows, breadth = features.shape
    me = lax.axis_index("veh")
    veh_here = me * local + jnp.arange(local)
    present = (veh_here < counts[0]) & (veh_here != ego_ids[0])
    live_count = jnp.where(present, req_count[0], 0)
    asked = (req_tiles[0][:, :, None] == (jnp.arange(breadth) // TILE)[None, None, :]) & (
        jnp.arange(KMAX)[None, :, None] < live_count[:, None, None]
    )
    live = jnp.sum(asked.astype(F32), axis=1)
    live = lax.all_gather(live, "veh", axis=0, tiled=True)
    half = cotangent.shape[2]
    cot = lax.all_gather(cotangent.reshape(1, channels * half, breadth), "veh", axis=0, tiled=True)
    x = features.reshape(local, channels * rows, breadth)
    enc_w = enc_weight.reshape(9 * channels, channels)
    post_w = post_weight.reshape(9 * channels, channels)
    pre, encoded = encode(x, enc_w)
    enc_all = lax.all_gather(encoded, "veh", axis=0, tiled=True)
    ids = jnp.stack([ego_ids[0], me]).astype(jnp.int32)
    embed = jnp.broadcast_to(ego_embed.astype(F32)[:, None], (channels, LANES))
    refined, post_part, eg = post(ids, enc_all, live, embed, cot, post_w, local)
    scene_bits = [("scene", b) for b in range(lax.axis_size("scene").bit_length() - 1)]
    veh_bits = [("veh", b) for b in range(lax.axis_size("veh").bit_length() - 1)]
    one = veh_bits + scene_bits
    two = veh_bits + scene_bits[1:2] + scene_bits[:1] + scene_bits[2:]
    fg, enc_part = back(x, pre, eg, enc_w)
    parts = jnp.concatenate([post_part, enc_part], axis=0)
    cut = parts.shape[0] // 2
    sums = jnp.concatenate(
        [sum_over_devices(parts[:cut], one), sum_over_devices(parts[cut:], two)], axis=0
    )
    post_sum, enc_sum = sums[: post_part.shape[0]], sums[post_part.shape[0] :]
    return (
        refined.reshape(batch, channels, half, breadth),
        fg.reshape(features.shape),
        enc_sum.reshape(enc_weight.shape),
        post_sum[: 9 * channels].reshape(post_weight.shape),
        post_sum[9 * channels],
    )


def solution(mesh):
    in_specs = (
        P("scene", "veh", None, None, None),
        P("scene"),
        P("scene"),
        P("scene", "veh", None),
        P("scene", "veh"),
        P(),
        P(),
        P(),
        P("scene", None, "veh", None),
    )
    out_specs = (P("scene", None, "veh", None), P("scene", "veh", None, None, None), P(), P(), P())
    return jax.shard_map(body, mesh=mesh, in_specs=in_specs, out_specs=out_specs, check_vma=False)
```
